32 devices in a mesh: dp: 8 (over z, core), mp: 4 (over y, x).
Axes of the slice: x: 2, y: 2, z: 4, core: 2. Of those that a mesh axis runs over, the one named last changes fastest.
Arguments:
- out_grad: bfloat16 [4096, 4096], P(('dp', 'mp')), may hold values from -6 to 6
- gate_pre: bfloat16 [4096, 14336], P('dp', 'mp'), may hold values from -6 to 6
- up_pre: bfloat16 [4096, 14336], P('dp', 'mp'), may hold values from -6 to 6
- down_weight: bfloat16 [14336, 4096], P('mp', 'dp'), may hold values from -0.046875 to 0.046875
Outputs:
- grad_gate_pre: bfloat16 [4096, 14336], P('dp', 'mp')
- grad_up_pre: bfloat16 [4096, 14336], P('dp', 'mp')
- grad_down: bfloat16 [14336, 4096], P('mp', 'dp')
The draws below stay inside these ranges and needn't reach their ends.
All inputs are finite; a program needn't handle non-finite values.
Results may differ from the reference program's by a relative error of at most 0.022.
Values may be sent and summed in bfloat16 or wider, within the bound.
No kernel may reach another device: no remote copies, remote signals or barrier semaphores. Data moves between devices by JAX's collectives and lax.ppermute only.
A program may use at most 128 MiB of HBM per device.

```python
import math
import jax
import jax.numpy as jnp
from jax import lax

D = 4096
FF = 14336
TOK_DEV = 128
TOKENS = 4096
N_DP = 8
N_MP = 4


def spiked(array, stream_key, source, target, shards_of, factor):
    def block_of(axis_at):
        return (jnp.arange(array.shape[axis_at]) // (array.shape[axis_at] // shards_of)).reshape((-1,) + (1,) * (array.ndim - 1 - axis_at))

    one_side = jax.random.permutation(stream_key, shards_of)[block_of(target)]
    second = (block_of(target) + shards_of // 2) % shards_of
    return jnp.where((block_of(source) == one_side) | (block_of(source) == second), factor * array, array)


def shard_levels(rng, shape, split, smallest, largest):
    def one(position, parts):
        steps = jax.random.uniform(jax.random.fold_in(jax.random.fold_in(rng, 6), position), (parts,), jnp.float32, smallest / len(split), largest / len(split))
        return jnp.repeat(jnp.exp(steps), shape[position] // parts).reshape((-1,) + (1,) * (len(shape) - position - 1))

    loudness = one(*split[0])
    for cut in split[1:]:
        loudness = loudness * one(*cut)
    return loudness


def gaussian(own_key, dims, deviation, most, split=(), dtype=jnp.bfloat16):
    result = jax.random.normal(own_key, dims, jnp.float32) * deviation
    if len(split) > 0:
        result = shard_levels(own_key, dims, split, -0.22, 0.18) * result
    return jnp.clip(result, min=-most, max=most).astype(dtype)


def bell_draw_with(stream_key, extent, spread, limit, cuts, heavy, kind=jnp.bfloat16):
    result = spread * jax.random.normal(stream_key, extent, jnp.float32)
    if cuts:
        result = result * shard_levels(stream_key, extent, cuts, -0.22, 0.18)
    return jnp.clip(spiked(result, jax.random.fold_in(stream_key, 3), *heavy), -limit, limit).astype(kind)


def setup_inputs(seed: int = 0) -> dict:
    streams_of = jax.random.split(jax.random.key(seed), 5)
    out_grad = bell_draw_with(streams_of[0], (TOKENS, D), 1.0, 6.0, ((0, 32),), (0, 1, 32, 2.75))
    gate_pre = gaussian(streams_of[1], (TOKENS, FF), 1.0, 6.0, ((0, 8), (1, 4)))
    up_pre = gaussian(streams_of[2], (TOKENS, FF), 1.0, 6.0, ((0, 8), (1, 4)))
    down_weight = gaussian(streams_of[3], (FF, D), FF ** -0.5, 0.046875, ((0, 4), (1, 8)))
    return {"out_grad": out_grad, "gate_pre": gate_pre, "up_pre": up_pre, "down_weight": down_weight}


def reference(out_grad, gate_pre, up_pre, down_weight):
    rows = TOK_DEV * N_MP
    grads = out_grad.reshape(N_DP, rows, D)
    gates = gate_pre.reshape(N_DP, rows, FF)
    ups = up_pre.reshape(N_DP, rows, FF)

    def replica_step(total, pieces):
        grad_rows, gate_rows, up_rows = pieces
        gate_float = gate_rows.astype(jnp.float32)
        up_float = up_rows.astype(jnp.float32)
        sigmoid_gate = jax.nn.sigmoid(gate_float)
        silu_gate = gate_float * sigmoid_gate
        hidden = (silu_gate * up_float).astype(jnp.bfloat16)
        d_hidden = jnp.dot(grad_rows, down_weight.T, preferred_element_type=jnp.float32)
        grad_gate = (d_hidden * up_float * sigmoid_gate * (1.0 + gate_float * (1.0 - sigmoid_gate))).astype(jnp.bfloat16)
        grad_up = (d_hidden * silu_gate).astype(jnp.bfloat16)
        term = jnp.dot(hidden.T, grad_rows, preferred_element_type=jnp.float32)
        term = lax.optimization_barrier(term.astype(jnp.bfloat16)).astype(jnp.float32)
        return (total + term, (grad_gate, grad_up))
    total, (grad_gate, grad_up) = lax.scan(replica_step, jnp.zeros((FF, D), jnp.float32), (grads, gates, ups))
    grad_down = (total * (1.0 / math.sqrt(TOKENS))).astype(jnp.bfloat16)
    return (grad_gate.reshape(TOKENS, FF), grad_up.reshape(TOKENS, FF), grad_down)
```

```python
import functools
import math

import jax
import jax.numpy as jnp
from jax import lax
from jax.experimental import pallas as pl
from jax.experimental.pallas import tpu as pltpu
from jax.sharding import PartitionSpec as P

VMEM = 60 * 1024 * 1024
COPIES = 4
STEP_FLOPS = 2e9
F32, BF16 = jnp.float32, jnp.bfloat16
ANY = pl.BlockSpec(memory_space=pl.ANY)


def call(kernel, grid, in_specs, out_specs, out_shape, name, aliases=None, flops=0, scratch=()):
    return pl.pallas_call(
        kernel,
        grid_spec=pltpu.PrefetchScalarGridSpec(
            num_scalar_prefetch=1,
            grid=grid,
            in_specs=in_specs,
            out_specs=out_specs,
            scratch_shapes=scratch,
        ),
        out_shape=out_shape,
        input_output_aliases=aliases or {},
        compiler_params=pltpu.CompilerParams(
            vmem_limit_bytes=VMEM, dimension_semantics=("arbitrary",) * len(grid)
        ),
        cost_estimate=pl.CostEstimate(flops=int(flops), bytes_accessed=0, transcendentals=0),
        name=name,
    )


def column_tile(chunk, most=896):
    return max(t for t in range(128, most + 1, 128) if chunk % t == 0)


def dot(a, b, contract):
    return lax.dot_general(a, b, (contract, ((), ())), preferred_element_type=F32)


def half_kernel(flip, place, weight_ref, *rest):
    out_ref, held, load_sem, store_sem = rest[-4:]
    half = out_ref.shape[0]
    part = half // COPIES
    start = (place[1] ^ flip) * half

    def load(i):
        source = pl.multiple_of(start + i * part, part)
        here = pl.ds(i * part, part)
        return pltpu.make_async_copy(
            weight_ref.at[pl.ds(source, part), :], held.at[here, :], load_sem.at[i]
        )

    def store(i):
        here = pl.ds(i * part, part)
        return pltpu.make_async_copy(held.at[here, :], out_ref.at[here, :], store_sem.at[i])

    for i in range(COPIES):
        load(i).start()
    for i in range(COPIES):
        load(i).wait()
        store(i).start()
    for i in range(COPIES):
        store(i).wait()


def half_call(place, weight, flip, after):
    units, block = weight.shape
    half = units // 2
    return call(
        functools.partial(half_kernel, flip),
        (1,),
        [ANY] * (1 + len(after)),
        ANY,
        jax.ShapeDtypeStruct((half, block), BF16),
        "half",
        scratch=[
            pltpu.VMEM((half, block), BF16),
            pltpu.SemaphoreType.DMA((COPIES,)),
            pltpu.SemaphoreType.DMA((COPIES,)),
        ],
    )(place, weight, *after)


def hidden_kernel(place, gate_own, up_own, gate_sib, up_sib, out_ref):
    tokens = gate_own.shape[0]
    core = place[1]
    for at, gate_ref, up_ref in ((core, gate_own, up_own), (1 - core, gate_sib, up_sib)):
        gate = gate_ref[...].astype(F32)
        up = up_ref[...].astype(F32)
        hidden = gate * jax.nn.sigmoid(gate) * up
        start = pl.multiple_of(at * tokens, tokens)
        out_ref[:, pl.ds(start, tokens)] = hidden.T.astype(BF16)


def hidden_call(place, *arrays):
    tokens, units = arrays[0].shape
    tile = column_tile(units, 256)
    return call(
        hidden_kernel,
        (units // tile,),
        [pl.BlockSpec((tokens, tile), lambda i, s: (0, i))] * 4,
        pl.BlockSpec((tile, 2 * tokens), lambda i, s: (i, 0)),
        jax.ShapeDtypeStruct((units, 2 * tokens), BF16),
        "hidden",
    )(place, *arrays)


def along(place, flow, line):
    return jnp.where(place[1] == flow, place[0], line - 1 - place[0])


def term_specs(tile, tokens, block, first, ahead, line):
    def column(i, s):
        return 0, 2 * lax.rem(s[0] + ahead(s), line) + s[1]

    return [
        pl.BlockSpec((tile, tokens), lambda i, s: (first + i, 0)),
        pl.BlockSpec((tokens, block), column),
    ]


def step_kernel(flow, j, line, place, got_ref, hidden_ref, grad_ref, out_ref):
    at = along(place, flow, line)
    adds = at + j < line

    @pl.when(adds)
    def _():
        term = dot(hidden_ref[...], grad_ref[...], ((1,), (0,)))
        before = jnp.where(at > 0, got_ref[...].astype(F32), 0.0)
        out_ref[...] = (before + term).astype(BF16)

    @pl.when(jnp.logical_not(adds))
    def _():
        out_ref[...] = got_ref[...]


def step_call(place, got, hidden, grads, k, j, flow, line):
    chunk, block = got.shape
    tokens = hidden.shape[1]
    steps = 4
    tile = chunk // steps

    def ahead(s):
        return jnp.where(s[1] == flow, j, line - j)

    return call(
        functools.partial(step_kernel, flow, j, line),
        (steps,),
        [pl.BlockSpec((tile, block), lambda i, s: (i, 0))]
        + term_specs(tile, tokens, block, k * steps, ahead, line),
        pl.BlockSpec((tile, block), lambda i, s: (i, 0)),
        jax.ShapeDtypeStruct((chunk, block), BF16),
        "step",
        flops=STEP_FLOPS,
    )(place, got, hidden, grads)


def own_kernel(place, hidden_ref, grad_ref, *rest):
    rest[-1][...] = dot(hidden_ref[...], grad_ref[...], ((1,), (0,))).astype(BF16)


def own_call(place, hidden, grads, block, line, after):
    units, tokens = hidden.shape
    steps = 8
    tile = units // steps
    return call(
        own_kernel,
        (steps,),
        term_specs(tile, tokens, block, 0, lambda s: 0, line) + [ANY] * len(after),
        pl.BlockSpec((tile, block), lambda i, s: (i, 0)),
        jax.ShapeDtypeStruct((units, block), BF16),
        "own",
    )(place, hidden, grads, *after)


def final_kernel(scale, line, place, one_ref, two_ref, own_ref, *rest):
    at = along(place, 0, line)
    one = jnp.where(at > 0, one_ref[...].astype(F32), 0.0)
    two = jnp.where(at < line - 1, two_ref[...].astype(F32), 0.0)
    out_ref, token = rest[-2:]
    out_ref[...] = ((one + two + own_ref[...].astype(F32)) * scale).astype(BF16)
    token[...] = jnp.zeros_like(token)


def final_call(place, one, two, own, k, line, scale, before, after):
    chunk, block = one.shape
    steps = 4
    tile = chunk // steps
    got = pl.BlockSpec((tile, block), lambda i, s: (i, 0))
    here = pl.BlockSpec((tile, block), lambda i, s: (k * steps + i, 0))
    return call(
        functools.partial(final_kernel, scale, line),
        (steps,),
        [got, got, here] + [ANY] * len(before + after),
        [here, pl.BlockSpec((8, 128), lambda i, s: (0, 0))],
        [jax.ShapeDtypeStruct(own.shape, BF16), jax.ShapeDtypeStruct((8, 128), F32)],
        "final",
        {4: 0} if before else None,
    )(place, one, two, own, *before, *after)


def half_product(line, place, grads, weights):
    count = len(weights) // 2
    at = along(place, 0, line)
    d_hidden = None
    for chain in range(2):
        for slot in range(line):
            weight = weights[chain * count + max(0, 2 * slot - 1)][...]
            if slot:
                weight = jnp.where(at >= slot, weight, weights[chain * count + 2 * slot][...])
            part = dot(grads[chain * line + slot][...], weight, ((1,), (1,)))
            d_hidden = part if d_hidden is None else d_hidden + part
    return d_hidden


def store_grads(d_hidden, gate_ref, up_ref, gate_out, up_out):
    gate = gate_ref[...].astype(F32)
    up = up_ref[...].astype(F32)
    sig = jax.nn.sigmoid(gate)
    gate_out[...] = (d_hidden * up * sig * (1.0 + gate * (1.0 - sig))).astype(BF16)
    up_out[...] = (d_hidden * (gate * sig)).astype(BF16)


def product_kernel(line, count, place, *refs):
    d_hidden = half_product(line, place, refs[: 2 * line], refs[2 * line : 2 * line + count])
    out_ref, token = refs[-2:]
    out_ref[...] = d_hidden.astype(BF16)
    token[...] = jnp.zeros_like(token)


def grads_kernel(line, count, place, *refs):
    d_hidden = half_product(line, place, refs[: 2 * line], refs[2 * line : 2 * line + count])
    gate_ref, up_ref = refs[2 * line + count : 2 * line + count + 2]
    gate_out, up_out, token = refs[-3:]
    store_grads(d_hidden, gate_ref, up_ref, gate_out, up_out)
    token[...] = jnp.zeros_like(token)


def product_call(place, grads, weights, gate_up, flip, line, after):
    half, block = weights[0].shape
    tokens = grads.shape[0] // 2
    tile = column_tile(half, 512)
    steps = half // tile
    here = pl.BlockSpec((tokens, tile), lambda i, s: (0, s[1] * steps + i))

    def row_spec(chain, slot):
        def block_of(i, s):
            source = lax.rem(s[0] + jnp.where(s[1] == 0, line - slot, slot), line)
            return s[1] ^ flip, 2 * source + (s[1] ^ chain)

        return pl.BlockSpec((tokens, block), block_of)

    def weight_spec(index):
        index = index % (2 * line - 1)
        slot, flow = (index + 1) // 2, (index + 1) % 2

        def block_of(i, s):
            if index == 0:
                return i, 0
            return jnp.where((along(s, 0, line) >= slot) == (flow == 0), i, 0), 0

        return pl.BlockSpec((tile, block), block_of)

    if gate_up:
        kernel, outs = grads_kernel, [here, here]
        shapes = [jax.ShapeDtypeStruct(gate_up[0].shape, BF16)] * 2
    else:
        kernel, outs = product_kernel, [pl.BlockSpec((tokens, tile), lambda i, s: (0, i))]
        shapes = [jax.ShapeDtypeStruct((tokens, half), BF16)]
    return call(
        functools.partial(kernel, line, len(weights)),
        (steps,),
        [row_spec(chain, slot) for chain in range(2) for slot in range(line)]
        + [weight_spec(index) for index in range(len(weights))]
        + [here] * len(gate_up)
        + [ANY] * len(after),
        outs + [pl.BlockSpec((8, 128), lambda i, s: (0, 0))],
        shapes + [jax.ShapeDtypeStruct((8, 128), F32)],
        "grads" if gate_up else "product",
    )(place, *[grads] * (2 * line), *weights, *gate_up, *after)


def join_kernel(place, product_ref, gate_ref, up_ref, *rest):
    gate_out, up_out = rest[-2:]
    store_grads(product_ref[...].astype(F32), gate_ref, up_ref, gate_out, up_out)


def join_call(place, product, gate, up, gate_all, up_all, after):
    tokens, half = product.shape
    tile = column_tile(half, 512)
    steps = half // tile
    there = pl.BlockSpec((tokens, tile), lambda i, s: (0, (1 - s[1]) * steps + i))
    return call(
        join_kernel,
        (steps,),
        [pl.BlockSpec((tokens, tile), lambda i, s: (0, i)), there, there, ANY, ANY]
        + [ANY] * len(after),
        [there, there],
        [jax.ShapeDtypeStruct(gate_all.shape, BF16)] * 2,
        "join",
        {4: 0, 5: 1},
    )(place, product, gate, up, gate_all, up_all, *after)


def shards(out_grad, gate_pre, up_pre, down_weight):
    n_dp, n_mp = lax.axis_size("dp"), lax.axis_size("mp")
    line = n_dp // 2
    rows, width = out_grad.shape
    tokens, units = gate_pre.shape
    block = down_weight.shape[1]
    scale = 1.0 / math.sqrt(rows * n_mp * n_dp)

    index = lax.axis_index("dp")
    place = jnp.stack([index // 2, index % 2]).astype(jnp.int32)
    swap_pairs = [(i, i ^ 1) for i in range(n_dp)]

    rings = []
    for flow in range(2):
        ring = [2 * z + flow for z in range(line)] + [2 * z + 1 - flow for z in reversed(range(line))]
        rings.append([(ring[i], ring[(i + 1) % n_dp]) for i in range(n_dp)])

    def swap(x):
        return lax.ppermute(x, "dp", swap_pairs)

    def send(x, flow):
        return lax.ppermute(x, "dp", rings[flow])

    half_own = half_call(place, down_weight, 0, ())
    first = [half_own, swap(half_call(place, down_weight, 1, (half_own,)))]
    got = [[[send(x, flow) for x in first]] for flow in range(2)]

    groups = [
        [(2 * z + c) * n_mp + m for c in range(2) for m in range(n_mp)] for z in range(line)
    ]
    out_grads = lax.all_gather(
        out_grad, ("dp", "mp"), axis=0, tiled=True, axis_index_groups=groups
    )
    gate_sib, up_sib = swap(gate_pre), swap(up_pre)
    hidden = hidden_call(place, gate_pre, up_pre, gate_sib, up_sib)

    sent = []
    for slot in range(2, line + 1):
        sent = [
            [
                step_call(place, got[flow][-1][k], hidden, out_grads, k, line + 1 - slot, flow, line)
                for k in range(2)
            ]
            for flow in range(2)
        ]
        for flow in range(2):
            got[flow].append([send(x, flow) for x in sent[flow]])
    sent = sent[0] + sent[1]
    own = own_call(place, hidden, out_grads, block, line, sent)

    weights = []
    for k in range(2):
        weights.append(first[k])
        for slot in range(1, line):
            weights += [got[0][slot - 1][k], got[1][line - slot - 1][k]]
    product, token = product_call(place, out_grads, weights, (), 1, line, sent)
    from_sib = swap(product)
    own_half = (gate_pre, up_pre)
    *grads, token = product_call(place, out_grads, weights, own_half, 0, line, [token])

    last = [got[flow][-1] for flow in range(2)]
    grad_down, token = final_call(place, last[0][0], last[1][0], own, 0, line, scale, (), (token,))
    grads = join_call(place, from_sib, gate_pre, up_pre, *grads, [token])
    grad_down, _ = final_call(
        place, last[0][1], last[1][1], own, 1, line, scale, (grad_down,), tuple(grads)
    )
    return (*grads, grad_down)


def solution(mesh):
    return jax.shard_map(
        shards,
        mesh=mesh,
        in_specs=(P(("dp", "mp"), None), P("dp", "mp"), P("dp", "mp"), P("mp", "dp")),
        out_specs=(P("dp", "mp"), P("dp", "mp"), P("mp", "dp")),
        check_vma=False,
    )
```

```python
import functools
import math

import jax
import jax.numpy as jnp
from jax import lax
from jax.experimental import pallas as pl
from jax.experimental.pallas import tpu as pltpu
from jax.sharding import PartitionSpec as P

VMEM = 60 * 1024 * 1024
COPIES = 4
STEP_FLOPS = 2e9
F32, BF16 = jnp.float32, jnp.bfloat16
ANY = pl.BlockSpec(memory_space=pl.ANY)


def call(kernel, grid, in_specs, out_specs, out_shape, name, aliases=None, flops=0, scratch=()):
    return pl.pallas_call(
        kernel,
        grid_spec=pltpu.PrefetchScalarGridSpec(
            num_scalar_prefetch=1,
            grid=grid,
            in_specs=in_specs,
            out_specs=out_specs,
            scratch_shapes=scratch,
        ),
        out_shape=out_shape,
        input_output_aliases=aliases or {},
        compiler_params=pltpu.CompilerParams(
            vmem_limit_bytes=VMEM, dimension_semantics=("arbitrary",) * len(grid)
        ),
        cost_estimate=pl.CostEstimate(flops=int(flops), bytes_accessed=0, transcendentals=0),
        name=name,
    )


def column_tile(chunk, most=896):
    return max(t for t in range(128, most + 1, 128) if chunk % t == 0)


def dot(a, b, contract):
    return lax.dot_general(a, b, (contract, ((), ())), preferred_element_type=F32)


def half_kernel(place, weight_ref, out_ref, held, load_sem, store_sem):
    half = out_ref.shape[0]
    part = half // COPIES
    start = place[1] * half

    def load(i):
        source = pl.multiple_of(start + i * part, part)
        here = pl.ds(i * part, part)
        return pltpu.make_async_copy(
            weight_ref.at[pl.ds(source, part), :], held.at[here, :], load_sem.at[i]
        )

    def store(i):
        here = pl.ds(i * part, part)
        return pltpu.make_async_copy(held.at[here, :], out_ref.at[here, :], store_sem.at[i])

    for i in range(COPIES):
        load(i).start()
    for i in range(COPIES):
        load(i).wait()
        store(i).start()
    for i in range(COPIES):
        store(i).wait()


def half_call(place, weight):
    units, block = weight.shape
    half = units // 2
    return call(
        half_kernel,
        (1,),
        [ANY],
        ANY,
        jax.ShapeDtypeStruct((half, block), BF16),
        "half",
        scratch=[
            pltpu.VMEM((half, block), BF16),
            pltpu.SemaphoreType.DMA((COPIES,)),
            pltpu.SemaphoreType.DMA((COPIES,)),
        ],
    )(place, weight)


def hidden_kernel(place, gate_own, up_own, gate_sib, up_sib, out_ref):
    tokens = gate_own.shape[0]
    core = place[1]
    for at, gate_ref, up_ref in ((core, gate_own, up_own), (1 - core, gate_sib, up_sib)):
        gate = gate_ref[...].astype(F32)
        up = up_ref[...].astype(F32)
        hidden = gate * jax.nn.sigmoid(gate) * up
        start = pl.multiple_of(at * tokens, tokens)
        out_ref[:, pl.ds(start, tokens)] = hidden.T.astype(BF16)


def hidden_call(place, *arrays):
    tokens, units = arrays[0].shape
    tile = column_tile(units, 256)
    return call(
        hidden_kernel,
        (units // tile,),
        [pl.BlockSpec((tokens, tile), lambda i, s: (0, i))] * 4,
        pl.BlockSpec((tile, 2 * tokens), lambda i, s: (i, 0)),
        jax.ShapeDtypeStruct((units, 2 * tokens), BF16),
        "hidden",
    )(place, *arrays)


def along(place, flow, line):
    return jnp.where(place[1] == flow, place[0], line - 1 - place[0])


def term_specs(tile, tokens, block, first, ahead, line):
    def column(i, s):
        return 0, 2 * lax.rem(s[0] + ahead(s), line) + s[1]

    return [
        pl.BlockSpec((tile, tokens), lambda i, s: (first + i, 0)),
        pl.BlockSpec((tokens, block), column),
    ]


def step_kernel(flow, j, line, place, got_ref, hidden_ref, grad_ref, *rest):
    out_ref = rest[-1]
    at = along(place, flow, line)
    adds = at + j < line

    @pl.when(adds)
    def _():
        term = dot(hidden_ref[...], grad_ref[...], ((1,), (0,)))
        before = jnp.where(at > 0, got_ref[...].astype(F32), 0.0)
        out_ref[...] = (before + term).astype(BF16)

    @pl.when(jnp.logical_not(adds))
    def _():
        out_ref[...] = got_ref[...]


def step_call(place, got, hidden, grads, k, quarters, j, flow, line, after=()):
    chunk, block = got.shape
    tokens = hidden.shape[1]
    tile = chunk // 4
    low, high = quarters

    def ahead(s):
        return jnp.where(s[1] == flow, j, line - j)

    return call(
        functools.partial(step_kernel, flow, j, line),
        (high - low,),
        [pl.BlockSpec((tile, block), lambda i, s: (low + i, 0))]
        + term_specs(tile, tokens, block, k * 4 + low, ahead, line)
        + [ANY] * len(after),
        pl.BlockSpec((tile, block), lambda i, s: (i, 0)),
        jax.ShapeDtypeStruct(((high - low) * tile, block), BF16),
        "step",
        flops=STEP_FLOPS * (high - low) / 4,
    )(place, got, hidden, grads, *after)


def own_kernel(place, hidden_ref, grad_ref, out_ref):
    out_ref[...] = dot(hidden_ref[...], grad_ref[...], ((1,), (0,))).astype(BF16)


def own_call(place, hidden, grads, block, line):
    units, tokens = hidden.shape
    steps = 8
    tile = units // steps
    return call(
        own_kernel,
        (steps,),
        term_specs(tile, tokens, block, 0, lambda s: 0, line),
        pl.BlockSpec((tile, block), lambda i, s: (i, 0)),
        jax.ShapeDtypeStruct((units, block), BF16),
        "own",
    )(place, hidden, grads)


def final_kernel(scale, line, place, one_ref, two_ref, own_ref, *rest):
    at = along(place, 0, line)
    out_ref, token = rest[-2:]
    token[...] = jnp.zeros_like(token)

    def store(*refs):
        total = own_ref[...].astype(F32)
        for ref in refs:
            total += ref[...].astype(F32)
        out_ref[...] = (total * scale).astype(BF16)

    @pl.when(at == 0)
    def _():
        store(two_ref)

    @pl.when(at == line - 1)
    def _():
        store(one_ref)

    @pl.when(jnp.logical_and(at > 0, at < line - 1))
    def _():
        store(one_ref, two_ref)


def final_call(place, one, two, own, quarter, line, scale, before, after):
    rows, block = one.shape
    tile = own.shape[0] // 16
    got = pl.BlockSpec((tile, block), lambda i, s: (i, 0))
    here = pl.BlockSpec((tile, block), lambda i, s: (2 * quarter + i, 0))
    return call(
        functools.partial(final_kernel, scale, line),
        (rows // tile,),
        [got, got, here] + [ANY] * len(before + after),
        [here, pl.BlockSpec((8, 128), lambda i, s: (0, 0))],
        [jax.ShapeDtypeStruct(own.shape, BF16), jax.ShapeDtypeStruct((8, 128), F32)],
        "final",
        {4: 0} if before else None,
    )(place, one, two, own, *before, *after)


def half_product(line, place, grads, weights):
    count = len(weights) // 2
    at = along(place, 0, line)
    d_hidden = None
    for chain in range(2):
        for slot in range(line):
            weight = weights[chain * count + max(0, 2 * slot - 1)][...]
            if slot:
                weight = jnp.where(at >= slot, weight, weights[chain * count + 2 * slot][...])
            part = dot(grads[chain * line + slot][...], weight, ((1,), (1,)))
            d_hidden = part if d_hidden is None else d_hidden + part
    return d_hidden


def store_grads(d_hidden, gate_ref, up_ref, gate_out, up_out):
    gate = gate_ref[...].astype(F32)
    up = up_ref[...].astype(F32)
    sig = jax.nn.sigmoid(gate)
    gate_out[...] = (d_hidden * up * sig * (1.0 + gate * (1.0 - sig))).astype(BF16)
    up_out[...] = (d_hidden * (gate * sig)).astype(BF16)


def product_kernel(line, count, place, *refs):
    d_hidden = half_product(line, place, refs[: 2 * line], refs[2 * line : 2 * line + count])
    out_ref, token = refs[-2:]
    out_ref[...] = d_hidden.astype(BF16)
    token[...] = jnp.zeros_like(token)


def grads_kernel(line, count, place, *refs):
    d_hidden = half_product(line, place, refs[: 2 * line], refs[2 * line : 2 * line + count])
    gate_ref, up_ref = refs[2 * line + count : 2 * line + count + 2]
    gate_out, up_out, token = refs[-3:]
    store_grads(d_hidden, gate_ref, up_ref, gate_out, up_out)
    token[...] = jnp.zeros_like(token)


def product_call(place, grads, weights, gate_up, flip, line, after):
    half, block = weights[0].shape
    tokens = grads.shape[0] // 2
    tile = column_tile(half, 512)
    steps = half // tile
    here = pl.BlockSpec((tokens, tile), lambda i, s: (0, s[1] * steps + i))

    def row_spec(chain, slot):
        def block_of(i, s):
            source = lax.rem(s[0] + jnp.where(s[1] == 0, line - slot, slot), line)
            return s[1] ^ flip, 2 * source + (s[1] ^ chain)

        return pl.BlockSpec((tokens, block), block_of)

    def weight_spec(index):
        index = index % (2 * line - 1)
        slot, flow = (index + 1) // 2, (index + 1) % 2

        def block_of(i, s):
            if index == 0:
                return i, 0
            return jnp.where((along(s, 0, line) >= slot) == (flow == 0), i, 0), 0

        return pl.BlockSpec((tile, block), block_of)

    if gate_up:
        kernel, outs = grads_kernel, [here, here]
        shapes = [jax.ShapeDtypeStruct(gate_up[0].shape, BF16)] * 2
    else:
        kernel, outs = product_kernel, [pl.BlockSpec((tokens, tile), lambda i, s: (0, i))]
        shapes = [jax.ShapeDtypeStruct((tokens, half), BF16)]
    return call(
        functools.partial(kernel, line, len(weights)),
        (steps,),
        [row_spec(chain, slot) for chain in range(2) for slot in range(line)]
        + [weight_spec(index) for index in range(len(weights))]
        + [here] * len(gate_up)
        + [ANY] * len(after),
        outs + [pl.BlockSpec((8, 128), lambda i, s: (0, 0))],
        shapes + [jax.ShapeDtypeStruct((8, 128), F32)],
        "grads" if gate_up else "product",
    )(place, *[grads] * (2 * line), *weights, *gate_up, *after)


def join_kernel(place, product_ref, gate_ref, up_ref, *rest):
    gate_out, up_out = rest[-2:]
    store_grads(product_ref[...].astype(F32), gate_ref, up_ref, gate_out, up_out)


def join_call(place, product, gate, up, gate_all, up_all, after):
    tokens, half = product.shape
    tile = column_tile(half, 512)
    steps = half // tile
    there = pl.BlockSpec((tokens, tile), lambda i, s: (0, (1 - s[1]) * steps + i))
    return call(
        join_kernel,
        (steps,),
        [pl.BlockSpec((tokens, tile), lambda i, s: (0, i)), there, there, ANY, ANY]
        + [ANY] * len(after),
        [there, there],
        [jax.ShapeDtypeStruct(gate_all.shape, BF16)] * 2,
        "join",
        {4: 0, 5: 1},
    )(place, product, gate, up, gate_all, up_all, *after)


def shards(out_grad, gate_pre, up_pre, down_weight):
    n_dp, n_mp = lax.axis_size("dp"), lax.axis_size("mp")
    line = n_dp // 2
    rows, width = out_grad.shape
    tokens, units = gate_pre.shape
    block = down_weight.shape[1]
    scale = 1.0 / math.sqrt(rows * n_mp * n_dp)

    index = lax.axis_index("dp")
    place = jnp.stack([index // 2, index % 2]).astype(jnp.int32)
    swap_pairs = [(i, i ^ 1) for i in range(n_dp)]

    rings = []
    for flow in range(2):
        ring = [2 * z + flow for z in range(line)] + [2 * z + 1 - flow for z in reversed(range(line))]
        rings.append([(ring[i], ring[(i + 1) % n_dp]) for i in range(n_dp)])

    def swap(x):
        return lax.ppermute(x, "dp", swap_pairs)

    def send(x, flow):
        return lax.ppermute(x, "dp", rings[flow])

    first = [half_call(place, down_weight), half_call(place, swap(down_weight))]
    got = [[[send(x, flow) for x in first]] for flow in range(2)]

    groups = [
        [(2 * z + c) * n_mp + m for c in range(2) for m in range(n_mp)] for z in range(line)
    ]
    out_grads = lax.all_gather(
        out_grad, ("dp", "mp"), axis=0, tiled=True, axis_index_groups=groups
    )
    gate_sib, up_sib = swap(gate_pre), swap(up_pre)
    hidden = hidden_call(place, gate_pre, up_pre, gate_sib, up_sib)

    def step(slot, flow, k, quarters, after=()):
        before = got[flow][slot - 2][k]
        j = line + 1 - slot
        return step_call(place, before, hidden, out_grads, k, quarters, j, flow, line, after)

    for slot in range(2, line):
        sent = [[step(slot, flow, k, (0, 4)) for k in range(2)] for flow in range(2)]
        for flow in range(2):
            got[flow].append([send(x, flow) for x in sent[flow]])

    own = own_call(place, hidden, out_grads, block, line)
    sent = [
        [step(line, flow, 0, (0, 4), (own,)), step(line, flow, 1, (0, 3))] for flow in range(2)
    ]
    last = [[send(x, flow) for x in sent[flow]] for flow in range(2)]
    sent = sent[0] + sent[1]

    weights = []
    for k in range(2):
        weights.append(first[k])
        for slot in range(1, line):
            weights += [got[0][slot - 1][k], got[1][line - slot - 1][k]]
    product, token = product_call(place, out_grads, weights, (), 1, line, sent)
    from_sib = swap(product)
    own_half = (gate_pre, up_pre)
    *grads, token = product_call(place, out_grads, weights, own_half, 0, line, [token])

    for flow in range(2):
        last[flow].append(send(step(line, flow, 1, (3, 4), (token,)), flow))
    one, two = last
    grad_down, token = final_call(place, one[0], two[0], own, 0, line, scale, (), (token,))
    grads = join_call(place, from_sib, gate_pre, up_pre, *grads, [token])
    for piece, quarter in ((1, 4), (2, 7)):
        grad_down, _ = final_call(
            place, one[piece], two[piece], own, quarter, line, scale, (grad_down,), tuple(grads)
        )
    return (*grads, grad_down)


def solution(mesh):
    return jax.shard_map(
        shards,
        mesh=mesh,
        in_specs=(P(("dp", "mp"), None), P("dp", "mp"), P("dp", "mp"), P("mp", "dp")),
        out_specs=(P("dp", "mp"), P("dp", "mp"), P("mp", "dp")),
        check_vma=False,
    )
```

```python
import functools
import math

import jax
import jax.numpy as jnp
from jax import lax
from jax.experimental import pallas as pl
from jax.experimental.pallas import tpu as pltpu
from jax.sharding import PartitionSpec as P

VMEM = 60 * 1024 * 1024
STEP_FLOPS = 2e9
F32, BF16 = jnp.float32, jnp.bfloat16
ANY = pl.BlockSpec(memory_space=pl.ANY)


def call(kernel, grid, in_specs, out_specs, out_shape, name, aliases=None, flops=0):
    return pl.pallas_call(
        kernel,
        grid_spec=pltpu.PrefetchScalarGridSpec(
            num_scalar_prefetch=1,
            grid=grid,
            in_specs=in_specs,
            out_specs=out_specs,
        ),
        out_shape=out_shape,
        input_output_aliases=aliases or {},
        compiler_params=pltpu.CompilerParams(
            vmem_limit_bytes=VMEM, dimension_semantics=("arbitrary",) * len(grid)
        ),
        cost_estimate=pl.CostEstimate(flops=int(flops), bytes_accessed=0, transcendentals=0),
        name=name,
    )


def column_tile(chunk, most=896):
    return max(t for t in range(128, most + 1, 128) if chunk % t == 0)


def dot(a, b, contract):
    return lax.dot_general(a, b, (contract, ((), ())), preferred_element_type=F32)


def spread_kernel(place, even_ref, odd_ref, out_ref):
    peers = out_ref.shape[0] // 2
    for core, ref in enumerate((even_ref, odd_ref)):
        for peer in range(peers):
            out_ref[core * peers + peer] = ref[...]


def spread_call(place, out_grad, peers, line, block):
    rows = out_grad.shape[0]
    return call(
        spread_kernel,
        (line,),
        [
            pl.BlockSpec((rows, block), lambda b, s: (0, 2 * b)),
            pl.BlockSpec((rows, block), lambda b, s: (0, 2 * b + 1)),
        ],
        pl.BlockSpec((peers, rows, block), lambda b, s: (0, 0, b)),
        jax.ShapeDtypeStruct((peers, rows, line * block), BF16),
        "spread",
    )(place, out_grad, out_grad)


def hidden_kernel(place, gate_own, up_own, gate_sib, up_sib, out_ref):
    tokens = gate_own.shape[0]
    core = place[1]
    for at, gate_ref, up_ref in ((core, gate_own, up_own), (1 - core, gate_sib, up_sib)):
        gate = gate_ref[...].astype(F32)
        up = up_ref[...].astype(F32)
        hidden = gate * jax.nn.sigmoid(gate) * up
        start = pl.multiple_of(at * tokens, tokens)
        out_ref[:, pl.ds(start, tokens)] = hidden.T.astype(BF16)


def hidden_call(place, *arrays):
    tokens, units = arrays[0].shape
    tile = column_tile(units, 256)
    return call(
        hidden_kernel,
        (units // tile,),
        [pl.BlockSpec((tokens, tile), lambda i, s: (0, i))] * 4,
        pl.BlockSpec((tile, 2 * tokens), lambda i, s: (i, 0)),
        jax.ShapeDtypeStruct((units, 2 * tokens), BF16),
        "hidden",
    )(place, *arrays)


def along(place, flow, line):
    return jnp.where(place[1] == flow, place[0], line - 1 - place[0])


def term_specs(tile, tokens, block, first, ahead, line):
    def column(i, s):
        return 0, lax.rem(s[0] + ahead(s), line)

    return [
        pl.BlockSpec((tile, tokens), lambda i, s: (first + i, 0)),
        pl.BlockSpec((tokens, block), column),
    ]


def step_kernel(flow, j, line, place, got_ref, hidden_ref, grad_ref, *rest):
    out_ref = rest[-1]
    at = along(place, flow, line)
    adds = at + j < line

    @pl.when(adds)
    def _():
        term = dot(hidden_ref[...], grad_ref[...], ((1,), (0,)))
        before = jnp.where(at > 0, got_ref[...].astype(F32), 0.0)
        out_ref[...] = (before + term).astype(BF16)

    @pl.when(jnp.logical_not(adds))
    def _():
        out_ref[...] = got_ref[...]


def step_call(place, got, hidden, grads, k, quarters, j, flow, line, after=()):
    chunk, block = got.shape
    tokens = hidden.shape[1]
    tile = chunk // 4
    low, high = quarters

    def ahead(s):
        return jnp.where(s[1] == flow, j, line - j)

    return call(
        functools.partial(step_kernel, flow, j, line),
        (high - low,),
        [pl.BlockSpec((tile, block), lambda i, s: (low + i, 0))]
        + term_specs(tile, tokens, block, k * 4 + low, ahead, line)
        + [ANY] * len(after),
        pl.BlockSpec((tile, block), lambda i, s: (i, 0)),
        jax.ShapeDtypeStruct(((high - low) * tile, block), BF16),
        "step",
        flops=STEP_FLOPS * (high - low) / 4,
    )(place, got, hidden, grads, *after)


def own_kernel(place, hidden_ref, grad_ref, out_ref):
    out_ref[...] = dot(hidden_ref[...], grad_ref[...], ((1,), (0,))).astype(BF16)


def own_call(place, hidden, grads, block, line):
    units, tokens = hidden.shape
    steps = 8
    tile = units // steps
    return call(
        own_kernel,
        (steps,),
        term_specs(tile, tokens, block, 0, lambda s: 0, line),
        pl.BlockSpec((tile, block), lambda i, s: (i, 0)),
        jax.ShapeDtypeStruct((units, block), BF16),
        "own",
    )(place, hidden, grads)


def final_kernel(scale, line, place, one_ref, two_ref, own_ref, *rest):
    at = along(place, 0, line)
    out_ref, token = rest[-2:]
    token[...] = jnp.zeros_like(token)

    def store(*refs):
        total = own_ref[...].astype(F32)
        for ref in refs:
            total += ref[...].astype(F32)
        out_ref[...] = (total * scale).astype(BF16)

    @pl.when(at == 0)
    def _():
        store(two_ref)

    @pl.when(at == line - 1)
    def _():
        store(one_ref)

    @pl.when(jnp.logical_and(at > 0, at < line - 1))
    def _():
        store(one_ref, two_ref)


def final_call(place, one, two, own, quarter, line, scale, before, after):
    rows, block = one.shape
    tile = own.shape[0] // 8
    if rows == tile:
        tile //= 2
    first = quarter * (own.shape[0] // 8) // tile
    got = pl.BlockSpec((tile, block), lambda i, s: (i, 0))
    here = pl.BlockSpec((tile, block), lambda i, s: (first + i, 0))
    return call(
        functools.partial(final_kernel, scale, line),
        (rows // tile,),
        [got, got, here] + [ANY] * len(before + after),
        [here, pl.BlockSpec((8, 128), lambda i, s: (0, 0))],
        [jax.ShapeDtypeStruct(own.shape, BF16), jax.ShapeDtypeStruct((8, 128), F32)],
        "final",
        {4: 0} if before else None,
    )(place, one, two, own, *before, *after)


def half_product(line, slots, place, grads, weights, before):
    at = along(place, 0, line)
    d_hidden = before[...] if before is not None else None
    weights, grads = iter(weights), iter(grads)
    for _ in range(2):
        for slot in slots:
            weight = next(weights)[...]
            if slot:
                other = next(weights)
                weight = jnp.where(at >= slot, weight, other[...])
            part = dot(next(grads)[...], weight, ((1,), (1,)))
            d_hidden = part if d_hidden is None else d_hidden + part
    return d_hidden


def store_grads(d_hidden, gate_ref, up_ref, gate_out, up_out):
    gate = gate_ref[...].astype(F32)
    up = up_ref[...].astype(F32)
    sig = jax.nn.sigmoid(gate)
    gate_out[...] = (d_hidden * up * sig * (1.0 + gate * (1.0 - sig))).astype(BF16)
    up_out[...] = (d_hidden * (gate * sig)).astype(BF16)


def product_kernel(line, slots, counts, place, *refs):
    n_grads, n_weights, n_before, n_gate = counts
    grads, refs = refs[:n_grads], refs[n_grads:]
    weights, refs = refs[:n_weights], refs[n_weights:]
    before = refs[0] if n_before else None
    d_hidden = half_product(line, slots, place, grads, weights, before)
    gate_up = refs[n_before : n_before + n_gate]
    *outs, token = refs[-2 - (n_gate > 0) :]
    if gate_up:
        store_grads(d_hidden, *gate_up, *outs)
    else:
        outs[0][...] = d_hidden.astype(outs[0].dtype)
    token[...] = jnp.zeros_like(token)


def product_call(place, grads, weights, slots, before, gate_up, dtype, flip, line, name, after):
    half, block = weights[0].shape
    tokens = grads[0].shape[0] // 2
    tile = column_tile(half, 512)
    steps = half // tile
    here = pl.BlockSpec((tokens, tile), lambda i, s: (0, s[1] * steps + i))
    short = pl.BlockSpec((tokens, tile), lambda i, s: (0, i))

    def row_spec(slot):
        def block_of(i, s):
            source = lax.rem(s[0] + jnp.where(s[1] == 0, line - slot, slot), line)
            return s[1] ^ flip, source

        return pl.BlockSpec((tokens, block), block_of)

    def weight_spec(slot, flow):
        def block_of(i, s):
            return jnp.where((along(s, 0, line) >= slot) == (flow == 0), i, 0), 0

        return pl.BlockSpec((tile, block), block_of if slot else lambda i, s: (i, 0))

    weight_specs = []
    for _ in range(2):
        for slot in slots:
            weight_specs += [weight_spec(slot, flow) for flow in range(2 if slot else 1)]
    if gate_up:
        outs, shapes = [here, here], [jax.ShapeDtypeStruct(gate_up[0].shape, BF16)] * 2
    else:
        outs, shapes = [short], [jax.ShapeDtypeStruct((tokens, half), dtype)]
    row_specs = [row_spec(slot) for _ in range(2) for slot in slots]
    counts = (len(row_specs), len(weights), len(before), len(gate_up))
    return call(
        functools.partial(product_kernel, line, slots, counts),
        (steps,),
        row_specs
        + weight_specs
        + [short] * len(before)
        + [here] * len(gate_up)
        + [ANY] * len(after),
        outs + [pl.BlockSpec((8, 128), lambda i, s: (0, 0))],
        shapes + [jax.ShapeDtypeStruct((8, 128), F32)],
        name,
    )(place, *[grads[0]] * len(slots), *[grads[1]] * len(slots), *weights, *before, *gate_up, *after)


def join_kernel(place, product_ref, gate_ref, up_ref, *rest):
    gate_out, up_out = rest[-2:]
    store_grads(product_ref[...].astype(F32), gate_ref, up_ref, gate_out, up_out)


def join_call(place, product, gate, up, gate_all, up_all, after):
    tokens, half = product.shape
    tile = column_tile(half, 896)
    steps = half // tile
    there = pl.BlockSpec((tokens, tile), lambda i, s: (0, (1 - s[1]) * steps + i))
    return call(
        join_kernel,
        (steps,),
        [pl.BlockSpec((tokens, tile), lambda i, s: (0, i)), there, there, ANY, ANY]
        + [ANY] * len(after),
        [there, there],
        [jax.ShapeDtypeStruct(gate_all.shape, BF16)] * 2,
        "join",
        {4: 0, 5: 1},
    )(place, product, gate, up, gate_all, up_all, *after)


def shards(out_grad, gate_pre, up_pre, down_weight):
    n_dp, n_mp = lax.axis_size("dp"), lax.axis_size("mp")
    line = n_dp // 2
    rows, width = out_grad.shape
    tokens, units = gate_pre.shape
    block = down_weight.shape[1]
    scale = 1.0 / math.sqrt(rows * n_mp * n_dp)

    index = lax.axis_index("dp")
    place = jnp.stack([index // 2, index % 2]).astype(jnp.int32)
    swap_pairs = [(i, i ^ 1) for i in range(n_dp)]

    rings = []
    for flow in range(2):
        ring = [2 * z + flow for z in range(line)] + [2 * z + 1 - flow for z in reversed(range(line))]
        rings.append([(ring[i], ring[(i + 1) % n_dp]) for i in range(n_dp)])

    def swap(x):
        return lax.ppermute(x, "dp", swap_pairs)

    def send(x, flow):
        return lax.ppermute(x, "dp", rings[flow])

    half = units // 2

    def own_half(weight):
        return lax.dynamic_slice_in_dim(weight, index % 2 * half, half, axis=0)

    first = [own_half(down_weight), own_half(swap(down_weight))]
    got = [[[send(x, flow) for x in first]] for flow in range(2)]

    groups = [
        [(2 * z + c) * n_mp + m for c in range(2) for m in range(n_mp)] for z in range(line)
    ]
    spread = spread_call(place, out_grad, 2 * n_mp, line, block)
    out_grads = lax.all_to_all(
        spread, ("dp", "mp"), split_axis=0, concat_axis=0, tiled=True, axis_index_groups=groups
    ).reshape(2 * tokens, line * block)
    both_grads = (out_grads, swap(out_grads))
    gate_sib, up_sib = swap(gate_pre), swap(up_pre)
    hidden = hidden_call(place, gate_pre, up_pre, gate_sib, up_sib)

    def step(slot, flow, k, quarters, after=()):
        before = got[flow][slot - 2][k]
        j = line + 1 - slot
        return step_call(place, before, hidden, out_grads, k, quarters, j, flow, line, after)

    for slot in range(2, line):
        sent = [[step(slot, flow, k, (0, 4)) for k in range(2)] for flow in range(2)]
        for flow in range(2):
            got[flow].append([send(x, flow) for x in sent[flow]])

    def weights_of(slots):
        weights = []
        for k in range(2):
            for slot in slots:
                if slot:
                    weights += [got[0][slot - 1][k], got[1][line - slot - 1][k]]
                else:
                    weights.append(first[k])
        return weights

    early_slots = [slot for slot in range(line) if slot not in (1, line - 1)]
    late_slots = [slot for slot in range(line) if slot not in early_slots]
    early = [
        product_call(
            place, both_grads, weights_of(early_slots), early_slots, (), (), F32, flip, line, "early", ()
        )
        for flip in (1, 0)
    ]

    own = own_call(place, hidden, out_grads, block, line)
    sent = [
        [
            step(line, flow, 0, (0, 4), (own,)),
            step(line, flow, 1, (0, 3), (early[0][1], early[1][1])),
        ]
        for flow in range(2)
    ]
    last = [[send(x, flow) for x in sent[flow]] for flow in range(2)]
    sent = sent[0] + sent[1]

    late = weights_of(late_slots)
    product, token = product_call(
        place, both_grads, late, late_slots, (early[0][0],), (), BF16, 1, line, "product", sent
    )
    from_sib = swap(product)
    *grads, token = product_call(
        place, both_grads, late, late_slots, (early[1][0],), (gate_pre, up_pre), None, 0, line, "grads", [token]
    )

    for flow in range(2):
        last[flow].append(send(step(line, flow, 1, (3, 4), (token,)), flow))
    one, two = last
    grad_down, token = final_call(place, one[0], two[0], own, 0, line, scale, (), (token,))
    grads = join_call(place, from_sib, gate_pre, up_pre, *grads, [token])
    grad_down, _ = final_call(
        place, one[1], two[1], own, 4, line, scale, (grad_down,), tuple(grads)
    )
    at = along(place, 0, line)
    start = units - units // 8
    total = own[start:].astype(F32)
    total += jnp.where(at > 0, one[2].astype(F32), 0.0)
    total += jnp.where(at < line - 1, two[2].astype(F32), 0.0)
    piece = (total * scale).astype(BF16)
    grad_down = lax.dynamic_update_slice_in_dim(grad_down, piece, start, axis=0)
    return (*grads, grad_down)


def solution(mesh):
    return jax.shard_map(
        shards,
        mesh=mesh,
        in_specs=(P(("dp", "mp"), None), P("dp", "mp"), P("dp", "mp"), P("mp", "dp")),
        out_specs=(P("dp", "mp"), P("dp", "mp"), P("mp", "dp")),
        check_vma=False,
    )
```

```python
import functools
import math

import jax
import jax.numpy as jnp
from jax import lax
from jax.experimental import pallas as pl
from jax.experimental.pallas import tpu as pltpu
from jax.sharding import PartitionSpec as P

VMEM = 60 * 1024 * 1024
STEP_FLOPS, ARRIVED_FLOPS = 2e9, 7e9
F32, BF16 = jnp.float32, jnp.bfloat16
ANY = pl.BlockSpec(memory_space=pl.ANY)


def call(kernel, grid, in_specs, out_specs, out_shape, name, aliases=None, flops=0):
    return pl.pallas_call(
        kernel,
        grid_spec=pltpu.PrefetchScalarGridSpec(
            num_scalar_prefetch=1,
            grid=grid,
            in_specs=in_specs,
            out_specs=out_specs,
        ),
        out_shape=out_shape,
        input_output_aliases=aliases or {},
        compiler_params=pltpu.CompilerParams(
            vmem_limit_bytes=VMEM, dimension_semantics=("arbitrary",) * len(grid)
        ),
        cost_estimate=pl.CostEstimate(flops=int(flops), bytes_accessed=0, transcendentals=0),
        name=name,
    )


def column_tile(chunk, most=896):
    return max(t for t in range(128, most + 1, 128) if chunk % t == 0)


def dot(a, b, contract):
    return lax.dot_general(a, b, (contract, ((), ())), preferred_element_type=F32)


def spread_kernel(line, grad_ref, out_ref, held, load_sem, store_sem):
    peers = out_ref.shape[0]
    block = held.shape[1] // (2 * line)

    def load(b):
        here = pl.ds(b * block, block)
        return pltpu.make_async_copy(grad_ref.at[:, here], held.at[:, here], load_sem.at[b])

    def store(b, peer):
        here = pl.ds(b // 2 * block, block)
        return pltpu.make_async_copy(
            held.at[:, pl.ds(b * block, block)], out_ref.at[peer, :, here], store_sem.at[b, peer]
        )

    places = [
        (b, b % 2 * (peers // 2) + peer) for b in range(2 * line) for peer in range(peers // 2)
    ]
    for b in range(2 * line):
        load(b).start()
    for b in range(2 * line):
        load(b).wait()
        for place in places:
            if place[0] == b:
                store(*place).start()
    for place in places:
        store(*place).wait()


def spread_call(out_grad, peers, line):
    rows, width = out_grad.shape
    return pl.pallas_call(
        functools.partial(spread_kernel, line),
        in_specs=[ANY],
        out_specs=ANY,
        out_shape=jax.ShapeDtypeStruct((peers, rows, width // 2), BF16),
        scratch_shapes=[
            pltpu.VMEM((rows, width), BF16),
            pltpu.SemaphoreType.DMA((2 * line,)),
            pltpu.SemaphoreType.DMA((2 * line, peers)),
        ],
        compiler_params=pltpu.CompilerParams(vmem_limit_bytes=VMEM),
        cost_estimate=pl.CostEstimate(flops=0, bytes_accessed=0, transcendentals=0),
        name="spread",
    )(out_grad)


def hidden_kernel(place, gate_own, up_own, gate_sib, up_sib, out_ref):
    tokens = gate_own.shape[0]
    core = place[1]
    for at, gate_ref, up_ref in ((core, gate_own, up_own), (1 - core, gate_sib, up_sib)):
        gate = gate_ref[...].astype(F32)
        up = up_ref[...].astype(F32)
        hidden = gate * jax.nn.sigmoid(gate) * up
        start = pl.multiple_of(at * tokens, tokens)
        out_ref[:, pl.ds(start, tokens)] = hidden.T.astype(BF16)


def hidden_call(place, *arrays):
    tokens, units = arrays[0].shape
    tile = column_tile(units, 256)
    return call(
        hidden_kernel,
        (units // tile,),
        [pl.BlockSpec((tokens, tile), lambda i, s: (0, i))] * 4,
        pl.BlockSpec((tile, 2 * tokens), lambda i, s: (i, 0)),
        jax.ShapeDtypeStruct((units, 2 * tokens), BF16),
        "hidden",
    )(place, *arrays)


def along(place, flow, line):
    return jnp.where(place[1] == flow, place[0], line - 1 - place[0])


def term_specs(tile, tokens, block, first, ahead, line):
    def column(i, s):
        return 0, lax.rem(s[0] + ahead(s), line)

    return [
        pl.BlockSpec((tile, tokens), lambda i, s: (first + i, 0)),
        pl.BlockSpec((tokens, block), column),
    ]


def arrived_kernel(place, *refs):
    refs[-1][...] = jnp.zeros_like(refs[-1])


def arrived_call(place, arrays):
    return call(
        arrived_kernel,
        (1,),
        [ANY] * len(arrays),
        pl.BlockSpec((8, 128), lambda i, s: (0, 0)),
        jax.ShapeDtypeStruct((8, 128), F32),
        "arrived",
        flops=ARRIVED_FLOPS,
    )(place, *arrays)


def step_kernel(flow, j, line, place, got_ref, hidden_ref, grad_ref, *rest):
    out_ref = rest[-1]
    at = along(place, flow, line)
    adds = at + j < line

    @pl.when(adds)
    def _():
        term = dot(hidden_ref[...], grad_ref[...], ((1,), (0,)))
        before = jnp.where(at > 0, got_ref[...].astype(F32), 0.0)
        out_ref[...] = (before + term).astype(BF16)

    @pl.when(jnp.logical_not(adds))
    def _():
        out_ref[...] = got_ref[...]


def step_call(place, got, hidden, grads, k, quarters, j, flow, line, after=()):
    chunk, block = got.shape
    tokens = hidden.shape[1]
    tile = chunk // 4
    low, high = quarters

    def ahead(s):
        return jnp.where(s[1] == flow, j, line - j)

    return call(
        functools.partial(step_kernel, flow, j, line),
        (high - low,),
        [pl.BlockSpec((tile, block), lambda i, s: (low + i, 0))]
        + term_specs(tile, tokens, block, k * 4 + low, ahead, line)
        + [ANY] * len(after),
        pl.BlockSpec((tile, block), lambda i, s: (i, 0)),
        jax.ShapeDtypeStruct(((high - low) * tile, block), BF16),
        "step",
        flops=STEP_FLOPS * (high - low) / 4,
    )(place, got, hidden, grads, *after)


def own_kernel(place, hidden_ref, grad_ref, out_ref):
    out_ref[...] = dot(hidden_ref[...], grad_ref[...], ((1,), (0,))).astype(BF16)


def own_call(place, hidden, grads, block, line):
    units, tokens = hidden.shape
    steps = 8
    tile = units // steps
    return call(
        own_kernel,
        (steps,),
        term_specs(tile, tokens, block, 0, lambda s: 0, line),
        pl.BlockSpec((tile, block), lambda i, s: (i, 0)),
        jax.ShapeDtypeStruct((units, block), BF16),
        "own",
    )(place, hidden, grads)


def final_kernel(scale, line, place, one_ref, two_ref, own_ref, *rest):
    at = along(place, 0, line)
    out_ref, token = rest[-2:]
    token[...] = jnp.zeros_like(token)

    def store(*refs):
        total = own_ref[...].astype(F32)
        for ref in refs:
            total += ref[...].astype(F32)
        out_ref[...] = (total * scale).astype(BF16)

    @pl.when(at == 0)
    def _():
        store(two_ref)

    @pl.when(at == line - 1)
    def _():
        store(one_ref)

    @pl.when(jnp.logical_and(at > 0, at < line - 1))
    def _():
        store(one_ref, two_ref)


def final_call(place, one, two, own, quarter, line, scale, before, after):
    rows, block = one.shape
    tile = own.shape[0] // 8
    if rows == tile:
        tile //= 2
    first = quarter * (own.shape[0] // 8) // tile
    got = pl.BlockSpec((tile, block), lambda i, s: (i, 0))
    here = pl.BlockSpec((tile, block), lambda i, s: (first + i, 0))
    return call(
        functools.partial(final_kernel, scale, line),
        (rows // tile,),
        [got, got, here] + [ANY] * len(before + after),
        [here, pl.BlockSpec((8, 128), lambda i, s: (0, 0))],
        [jax.ShapeDtypeStruct(own.shape, BF16), jax.ShapeDtypeStruct((8, 128), F32)],
        "final",
        {4: 0} if before else None,
    )(place, one, two, own, *before, *after)


def half_product(line, slots, place, grads, weights, before):
    at = along(place, 0, line)
    d_hidden = before[...] if before is not None else None
    weights, grads = iter(weights), iter(grads)
    for _ in range(2):
        for slot in slots:
            weight = next(weights)[...]
            if slot:
                other = next(weights)
                weight = jnp.where(at >= slot, weight, other[...])
            part = dot(next(grads)[...], weight, ((1,), (1,)))
            d_hidden = part if d_hidden is None else d_hidden + part
    return d_hidden


def store_grads(d_hidden, gate_ref, up_ref, gate_out, up_out):
    gate = gate_ref[...].astype(F32)
    up = up_ref[...].astype(F32)
    sig = jax.nn.sigmoid(gate)
    gate_out[...] = (d_hidden * up * sig * (1.0 + gate * (1.0 - sig))).astype(BF16)
    up_out[...] = (d_hidden * (gate * sig)).astype(BF16)


def product_kernel(line, slots, counts, place, *refs):
    n_grads, n_weights, n_before, n_gate = counts
    grads, refs = refs[:n_grads], refs[n_grads:]
    weights, refs = refs[:n_weights], refs[n_weights:]
    before = refs[0] if n_before else None
    d_hidden = half_product(line, slots, place, grads, weights, before)
    gate_up = refs[n_before : n_before + n_gate]
    *outs, token = refs[-2 - (n_gate > 0) :]
    if gate_up:
        store_grads(d_hidden, *gate_up, *outs)
    else:
        outs[0][...] = d_hidden.astype(outs[0].dtype)
    token[...] = jnp.zeros_like(token)


def product_call(place, grads, weights, slots, before, gate_up, dtype, flip, line, name, after):
    half, block = weights[0].shape
    tokens = grads[0].shape[0] // 2
    tile = column_tile(half, 512)
    steps = half // tile
    here = pl.BlockSpec((tokens, tile), lambda i, s: (0, s[1] * steps + i))
    short = pl.BlockSpec((tokens, tile), lambda i, s: (0, i))

    def row_spec(slot):
        def block_of(i, s):
            source = lax.rem(s[0] + jnp.where(s[1] == 0, line - slot, slot), line)
            return s[1] ^ flip, source

        return pl.BlockSpec((tokens, block), block_of)

    def weight_spec(slot, flow):
        def block_of(i, s):
            return jnp.where((along(s, 0, line) >= slot) == (flow == 0), i, 0), 0

        return pl.BlockSpec((tile, block), block_of if slot else lambda i, s: (i, 0))

    weight_specs = []
    for _ in range(2):
        for slot in slots:
            weight_specs += [weight_spec(slot, flow) for flow in range(2 if slot else 1)]
    if gate_up:
        outs, shapes = [here, here], [jax.ShapeDtypeStruct(gate_up[0].shape, BF16)] * 2
    else:
        outs, shapes = [short], [jax.ShapeDtypeStruct((tokens, half), dtype)]
    row_specs = [row_spec(slot) for _ in range(2) for slot in slots]
    counts = (len(row_specs), len(weights), len(before), len(gate_up))
    return call(
        functools.partial(product_kernel, line, slots, counts),
        (steps,),
        row_specs
        + weight_specs
        + [short] * len(before)
        + [here] * len(gate_up)
        + [ANY] * len(after),
        outs + [pl.BlockSpec((8, 128), lambda i, s: (0, 0))],
        shapes + [jax.ShapeDtypeStruct((8, 128), F32)],
        name,
    )(place, *[grads[0]] * len(slots), *[grads[1]] * len(slots), *weights, *before, *gate_up, *after)


def join_kernel(place, product_ref, gate_ref, up_ref, *rest):
    gate_out, up_out = rest[-2:]
    store_grads(product_ref[...].astype(F32), gate_ref, up_ref, gate_out, up_out)


def join_call(place, product, gate, up, gate_all, up_all, after):
    tokens, half = product.shape
    tile = column_tile(half, 896)
    steps = half // tile
    there = pl.BlockSpec((tokens, tile), lambda i, s: (0, (1 - s[1]) * steps + i))
    return call(
        join_kernel,
        (steps,),
        [pl.BlockSpec((tokens, tile), lambda i, s: (0, i)), there, there, ANY, ANY]
        + [ANY] * len(after),
        [there, there],
        [jax.ShapeDtypeStruct(gate_all.shape, BF16)] * 2,
        "join",
        {4: 0, 5: 1},
    )(place, product, gate, up, gate_all, up_all, *after)


def shards(out_grad, gate_pre, up_pre, down_weight):
    n_dp, n_mp = lax.axis_size("dp"), lax.axis_size("mp")
    line = n_dp // 2
    rows, width = out_grad.shape
    tokens, units = gate_pre.shape
    block = down_weight.shape[1]
    scale = 1.0 / math.sqrt(rows * n_mp * n_dp)

    index = lax.axis_index("dp")
    place = jnp.stack([index // 2, index % 2]).astype(jnp.int32)
    swap_pairs = [(i, i ^ 1) for i in range(n_dp)]

    rings = []
    for flow in range(2):
        ring = [2 * z + flow for z in range(line)] + [2 * z + 1 - flow for z in reversed(range(line))]
        rings.append([(ring[i], ring[(i + 1) % n_dp]) for i in range(n_dp)])

    def swap(x):
        return lax.ppermute(x, "dp", swap_pairs)

    def send(x, flow):
        return lax.ppermute(x, "dp", rings[flow])

    half = units // 2

    def own_half(weight):
        return lax.dynamic_slice_in_dim(weight, index % 2 * half, half, axis=0)

    first = [own_half(down_weight), own_half(swap(down_weight))]
    got = [[[send(x, flow) for x in first]] for flow in range(2)]

    groups = [
        [(2 * z + c) * n_mp + m for c in range(2) for m in range(n_mp)] for z in range(line)
    ]
    spread = spread_call(out_grad, 2 * n_mp, line)
    out_grads = lax.all_to_all(
        spread, ("dp", "mp"), split_axis=0, concat_axis=0, tiled=True, axis_index_groups=groups
    ).reshape(2 * tokens, line * block)
    both_grads = (out_grads, swap(out_grads))
    gate_sib, up_sib = swap(gate_pre), swap(up_pre)
    hidden = hidden_call(place, gate_pre, up_pre, gate_sib, up_sib)

    def step(slot, flow, k, quarters, after=()):
        before = got[flow][slot - 2][k]
        j = line + 1 - slot
        return step_call(place, before, hidden, out_grads, k, quarters, j, flow, line, after)

    arrived = arrived_call(place, [got[flow][0][0] for flow in range(2)])
    for slot in range(2, line):
        after = [(arrived,) if slot == 2 else (), ()]
        sent = [[step(slot, flow, k, (0, 4), after[k]) for k in range(2)] for flow in range(2)]
        for flow in range(2):
            got[flow].append([send(x, flow) for x in sent[flow]])

    def weights_of(slots):
        weights = []
        for k in range(2):
            for slot in slots:
                if slot:
                    weights += [got[0][slot - 1][k], got[1][line - slot - 1][k]]
                else:
                    weights.append(first[k])
        return weights

    early_slots = [slot for slot in range(line) if slot not in (1, line - 1)]
    late_slots = [slot for slot in range(line) if slot not in early_slots]
    early = [
        product_call(
            place, both_grads, weights_of(early_slots), early_slots, (), (), F32, flip, line, "early", ()
        )
        for flip in (1, 0)
    ]

    own = own_call(place, hidden, out_grads, block, line)
    sent = [
        [
            step(line, flow, 0, (0, 4), (own,)),
            step(line, flow, 1, (0, 3), (early[0][1], early[1][1])),
        ]
        for flow in range(2)
    ]
    last = [[send(x, flow) for x in sent[flow]] for flow in range(2)]
    sent = sent[0] + sent[1]

    late = weights_of(late_slots)
    product, token = product_call(
        place, both_grads, late, late_slots, (early[0][0],), (), BF16, 1, line, "product", sent
    )
    from_sib = swap(product)
    *grads, token = product_call(
        place, both_grads, late, late_slots, (early[1][0],), (gate_pre, up_pre), None, 0, line, "grads", [token]
    )

    for flow in range(2):
        last[flow].append(send(step(line, flow, 1, (3, 4), (token,)), flow))
    one, two = last
    grad_down, token = final_call(place, one[0], two[0], own, 0, line, scale, (), (token,))
    grads = join_call(place, from_sib, gate_pre, up_pre, *grads, [token])
    grad_down, _ = final_call(
        place, one[1], two[1], own, 4, line, scale, (grad_down,), tuple(grads)
    )
    at = along(place, 0, line)
    start = units - units // 8
    total = own[start:].astype(F32)
    total += jnp.where(at > 0, one[2].astype(F32), 0.0)
    total += jnp.where(at < line - 1, two[2].astype(F32), 0.0)
    piece = (total * scale).astype(BF16)
    grad_down = lax.dynamic_update_slice_in_dim(grad_down, piece, start, axis=0)
    return (*grads, grad_down)


def solution(mesh):
    return jax.shard_map(
        shards,
        mesh=mesh,
        in_specs=(P(("dp", "mp"), None), P("dp", "mp"), P("dp", "mp"), P("mp", "dp")),
        out_specs=(P("dp", "mp"), P("dp", "mp"), P("mp", "dp")),
        check_vma=False,
    )
```

```python
import functools
import math

import jax
import jax.numpy as jnp
from jax import lax
from jax.experimental import pallas as pl
from jax.experimental.pallas import tpu as pltpu
from jax.sharding import PartitionSpec as P

VMEM = 60 * 1024 * 1024
STEP_FLOPS, ARRIVED_FLOPS = 2e9, 1.4e10
F32, BF16 = jnp.float32, jnp.bfloat16
ANY = pl.BlockSpec(memory_space=pl.ANY)


def call(kernel, grid, in_specs, out_specs, out_shape, name, aliases=None, flops=0):
    return pl.pallas_call(
        kernel,
        grid_spec=pltpu.PrefetchScalarGridSpec(
            num_scalar_prefetch=1,
            grid=grid,
            in_specs=in_specs,
            out_specs=out_specs,
        ),
        out_shape=out_shape,
        input_output_aliases=aliases or {},
        compiler_params=pltpu.CompilerParams(
            vmem_limit_bytes=VMEM, dimension_semantics=("arbitrary",) * len(grid)
        ),
        cost_estimate=pl.CostEstimate(flops=int(flops), bytes_accessed=0, transcendentals=0),
        name=name,
    )


def column_tile(chunk, most=896):
    return max(t for t in range(128, most + 1, 128) if chunk % t == 0)


def dot(a, b, contract):
    return lax.dot_general(a, b, (contract, ((), ())), preferred_element_type=F32)


def spread_kernel(line, grad_ref, out_ref, held, load_sem, store_sem):
    peers = out_ref.shape[0]
    block = held.shape[1] // (2 * line)

    def load(b):
        here = pl.ds(b * block, block)
        return pltpu.make_async_copy(grad_ref.at[:, here], held.at[:, here], load_sem.at[b])

    def store(b, peer):
        here = pl.ds(b // 2 * block, block)
        return pltpu.make_async_copy(
            held.at[:, pl.ds(b * block, block)], out_ref.at[peer, :, here], store_sem.at[b, peer]
        )

    places = [
        (b, b % 2 * (peers // 2) + peer) for b in range(2 * line) for peer in range(peers // 2)
    ]
    for b in range(2 * line):
        load(b).start()
    for b in range(2 * line):
        load(b).wait()
        for place in places:
            if place[0] == b:
                store(*place).start()
    for place in places:
        store(*place).wait()


def spread_call(out_grad, peers, line):
    rows, width = out_grad.shape
    return pl.pallas_call(
        functools.partial(spread_kernel, line),
        in_specs=[ANY],
        out_specs=ANY,
        out_shape=jax.ShapeDtypeStruct((peers, rows, width // 2), BF16),
        scratch_shapes=[
            pltpu.VMEM((rows, width), BF16),
            pltpu.SemaphoreType.DMA((2 * line,)),
            pltpu.SemaphoreType.DMA((2 * line, peers)),
        ],
        compiler_params=pltpu.CompilerParams(vmem_limit_bytes=VMEM),
        cost_estimate=pl.CostEstimate(flops=0, bytes_accessed=0, transcendentals=0),
        name="spread",
    )(out_grad)


def hidden_kernel(place, gate_own, up_own, gate_sib, up_sib, out_ref):
    tokens = gate_own.shape[0]
    core = place[1]
    for at, gate_ref, up_ref in ((core, gate_own, up_own), (1 - core, gate_sib, up_sib)):
        gate = gate_ref[...].astype(F32)
        up = up_ref[...].astype(F32)
        hidden = gate * jax.nn.sigmoid(gate) * up
        start = pl.multiple_of(at * tokens, tokens)
        out_ref[:, pl.ds(start, tokens)] = hidden.T.astype(BF16)


def hidden_call(place, *arrays):
    tokens, units = arrays[0].shape
    tile = column_tile(units, 256)
    return call(
        hidden_kernel,
        (units // tile,),
        [pl.BlockSpec((tokens, tile), lambda i, s: (0, i))] * 4,
        pl.BlockSpec((tile, 2 * tokens), lambda i, s: (i, 0)),
        jax.ShapeDtypeStruct((units, 2 * tokens), BF16),
        "hidden",
    )(place, *arrays)


def along(place, flow, line):
    return jnp.where(place[1] == flow, place[0], line - 1 - place[0])


def term_specs(tile, tokens, block, first, ahead, line):
    def column(i, s):
        return 0, lax.rem(s[0] + ahead(s), line)

    return [
        pl.BlockSpec((tile, tokens), lambda i, s: (first + i, 0)),
        pl.BlockSpec((tokens, block), column),
    ]


def arrived_kernel(place, *refs):
    refs[-1][...] = jnp.zeros_like(refs[-1])


def arrived_call(place, arrays):
    return call(
        arrived_kernel,
        (1,),
        [ANY] * len(arrays),
        pl.BlockSpec((8, 128), lambda i, s: (0, 0)),
        jax.ShapeDtypeStruct((8, 128), F32),
        "arrived",
        flops=ARRIVED_FLOPS,
    )(place, *arrays)


def step_kernel(flow, j, line, place, got_ref, hidden_ref, grad_ref, *rest):
    out_ref = rest[-1]
    at = along(place, flow, line)
    adds = at + j < line

    @pl.when(adds)
    def _():
        term = dot(hidden_ref[...], grad_ref[...], ((1,), (0,)))
        before = jnp.where(at > 0, got_ref[...].astype(F32), 0.0)
        out_ref[...] = (before + term).astype(BF16)

    @pl.when(jnp.logical_not(adds))
    def _():
        out_ref[...] = got_ref[...]


def step_call(place, got, hidden, grads, k, quarters, j, flow, line, after=()):
    chunk, block = got.shape
    tokens = hidden.shape[1]
    tile = chunk // 4
    low, high = quarters

    def ahead(s):
        return jnp.where(s[1] == flow, j, line - j)

    return call(
        functools.partial(step_kernel, flow, j, line),
        (high - low,),
        [pl.BlockSpec((tile, block), lambda i, s: (low + i, 0))]
        + term_specs(tile, tokens, block, k * 4 + low, ahead, line)
        + [ANY] * len(after),
        pl.BlockSpec((tile, block), lambda i, s: (i, 0)),
        jax.ShapeDtypeStruct(((high - low) * tile, block), BF16),
        "step",
        flops=STEP_FLOPS * (high - low) / 4,
    )(place, got, hidden, grads, *after)


def own_kernel(place, hidden_ref, grad_ref, out_ref):
    out_ref[...] = dot(hidden_ref[...], grad_ref[...], ((1,), (0,))).astype(BF16)


def own_call(place, hidden, grads, block, line):
    units, tokens = hidden.shape
    steps = 8
    tile = units // steps
    return call(
        own_kernel,
        (steps,),
        term_specs(tile, tokens, block, 0, lambda s: 0, line),
        pl.BlockSpec((tile, block), lambda i, s: (i, 0)),
        jax.ShapeDtypeStruct((units, block), BF16),
        "own",
    )(place, hidden, grads)


def final_kernel(scale, line, place, one_ref, two_ref, own_ref, *rest):
    at = along(place, 0, line)
    out_ref, token = rest[-2:]
    token[...] = jnp.zeros_like(token)

    def store(*refs):
        total = own_ref[...].astype(F32)
        for ref in refs:
            total += ref[...].astype(F32)
        out_ref[...] = (total * scale).astype(BF16)

    @pl.when(at == 0)
    def _():
        store(two_ref)

    @pl.when(at == line - 1)
    def _():
        store(one_ref)

    @pl.when(jnp.logical_and(at > 0, at < line - 1))
    def _():
        store(one_ref, two_ref)


def final_call(place, one, two, own, quarter, line, scale, before, after):
    rows, block = one.shape
    tile = own.shape[0] // 8
    if rows == tile:
        tile //= 2
    first = quarter * (own.shape[0] // 8) // tile
    got = pl.BlockSpec((tile, block), lambda i, s: (i, 0))
    here = pl.BlockSpec((tile, block), lambda i, s: (first + i, 0))
    return call(
        functools.partial(final_kernel, scale, line),
        (rows // tile,),
        [got, got, here] + [ANY] * len(before + after),
        [here, pl.BlockSpec((8, 128), lambda i, s: (0, 0))],
        [jax.ShapeDtypeStruct(own.shape, BF16), jax.ShapeDtypeStruct((8, 128), F32)],
        "final",
        {4: 0} if before else None,
    )(place, one, two, own, *before, *after)


def half_product(line, slots, place, grads, weights, before):
    at = along(place, 0, line)
    d_hidden = before[...] if before is not None else None
    weights, grads = iter(weights), iter(grads)
    for _ in range(2):
        for slot in slots:
            weight = next(weights)[...]
            if slot:
                other = next(weights)
                weight = jnp.where(at >= slot, weight, other[...])
            part = dot(next(grads)[...], weight, ((1,), (1,)))
            d_hidden = part if d_hidden is None else d_hidden + part
    return d_hidden


def store_grads(d_hidden, gate_ref, up_ref, gate_out, up_out):
    gate = gate_ref[...].astype(F32)
    up = up_ref[...].astype(F32)
    sig = jax.nn.sigmoid(gate)
    gate_out[...] = (d_hidden * up * sig * (1.0 + gate * (1.0 - sig))).astype(BF16)
    up_out[...] = (d_hidden * (gate * sig)).astype(BF16)


def product_kernel(line, slots, counts, place, *refs):
    n_grads, n_weights, n_before, n_gate = counts
    grads, refs = refs[:n_grads], refs[n_grads:]
    weights, refs = refs[:n_weights], refs[n_weights:]
    before = refs[0] if n_before else None
    d_hidden = half_product(line, slots, place, grads, weights, before)
    gate_up = refs[n_before : n_before + n_gate]
    *outs, token = refs[-2 - (n_gate > 0) :]
    if gate_up:
        store_grads(d_hidden, *gate_up, *outs)
    else:
        outs[0][...] = d_hidden.astype(outs[0].dtype)
    token[...] = jnp.zeros_like(token)


def product_call(place, grads, weights, slots, before, gate_up, dtype, flip, line, name, after):
    half, block = weights[0].shape
    tokens = grads[0].shape[0] // 2
    tile = column_tile(half, 512)
    steps = half // tile
    here = pl.BlockSpec((tokens, tile), lambda i, s: (0, s[1] * steps + i))
    short = pl.BlockSpec((tokens, tile), lambda i, s: (0, i))

    def row_spec(slot):
        def block_of(i, s):
            source = lax.rem(s[0] + jnp.where(s[1] == 0, line - slot, slot), line)
            return s[1] ^ flip, source

        return pl.BlockSpec((tokens, block), block_of)

    def weight_spec(slot, flow):
        def block_of(i, s):
            return jnp.where((along(s, 0, line) >= slot) == (flow == 0), i, 0), 0

        return pl.BlockSpec((tile, block), block_of if slot else lambda i, s: (i, 0))

    weight_specs = []
    for _ in range(2):
        for slot in slots:
            weight_specs += [weight_spec(slot, flow) for flow in range(2 if slot else 1)]
    if gate_up:
        outs, shapes = [here, here], [jax.ShapeDtypeStruct(gate_up[0].shape, BF16)] * 2
    else:
        outs, shapes = [short], [jax.ShapeDtypeStruct((tokens, half), dtype)]
    row_specs = [row_spec(slot) for _ in range(2) for slot in slots]
    counts = (len(row_specs), len(weights), len(before), len(gate_up))
    return call(
        functools.partial(product_kernel, line, slots, counts),
        (steps,),
        row_specs
        + weight_specs
        + [short] * len(before)
        + [here] * len(gate_up)
        + [ANY] * len(after),
        outs + [pl.BlockSpec((8, 128), lambda i, s: (0, 0))],
        shapes + [jax.ShapeDtypeStruct((8, 128), F32)],
        name,
    )(place, *[grads[0]] * len(slots), *[grads[1]] * len(slots), *weights, *before, *gate_up, *after)


def join_kernel(place, product_ref, gate_ref, up_ref, *rest):
    gate_out, up_out = rest[-2:]
    store_grads(product_ref[...].astype(F32), gate_ref, up_ref, gate_out, up_out)


def join_call(place, product, gate, up, gate_all, up_all, after):
    tokens, half = product.shape
    tile = column_tile(half, 896)
    steps = half // tile
    there = pl.BlockSpec((tokens, tile), lambda i, s: (0, (1 - s[1]) * steps + i))
    return call(
        join_kernel,
        (steps,),
        [pl.BlockSpec((tokens, tile), lambda i, s: (0, i)), there, there, ANY, ANY]
        + [ANY] * len(after),
        [there, there],
        [jax.ShapeDtypeStruct(gate_all.shape, BF16)] * 2,
        "join",
        {4: 0, 5: 1},
    )(place, product, gate, up, gate_all, up_all, *after)


def shards(out_grad, gate_pre, up_pre, down_weight):
    n_dp, n_mp = lax.axis_size("dp"), lax.axis_size("mp")
    line = n_dp // 2
    rows, width = out_grad.shape
    tokens, units = gate_pre.shape
    block = down_weight.shape[1]
    scale = 1.0 / math.sqrt(rows * n_mp * n_dp)

    index = lax.axis_index("dp")
    place = jnp.stack([index // 2, index % 2]).astype(jnp.int32)
    swap_pairs = [(i, i ^ 1) for i in range(n_dp)]

    rings = []
    for flow in range(2):
        ring = [2 * z + flow for z in range(line)] + [2 * z + 1 - flow for z in reversed(range(line))]
        rings.append([(ring[i], ring[(i + 1) % n_dp]) for i in range(n_dp)])

    def swap(x):
        return lax.ppermute(x, "dp", swap_pairs)

    def send(x, flow):
        return lax.ppermute(x, "dp", rings[flow])

    half = units // 2

    def own_half(weight):
        return lax.dynamic_slice_in_dim(weight, index % 2 * half, half, axis=0)

    first = [own_half(down_weight), own_half(swap(down_weight))]
    got = [[[send(x, flow) for x in first]] for flow in range(2)]

    groups = [
        [(2 * z + c) * n_mp + m for c in range(2) for m in range(n_mp)] for z in range(line)
    ]
    spread = spread_call(out_grad, 2 * n_mp, line)
    out_grads = lax.all_to_all(
        spread, ("dp", "mp"), split_axis=0, concat_axis=0, tiled=True, axis_index_groups=groups
    ).reshape(2 * tokens, line * block)
    both_grads = (out_grads, swap(out_grads))
    gate_sib, up_sib = swap(gate_pre), swap(up_pre)
    hidden = hidden_call(place, gate_pre, up_pre, gate_sib, up_sib)

    def step(slot, flow, k, quarters, after=()):
        before = got[flow][slot - 2][k]
        j = line + 1 - slot
        return step_call(place, before, hidden, out_grads, k, quarters, j, flow, line, after)

    arrived = arrived_call(place, [got[flow][0][0] for flow in range(2)])
    for slot in range(2, line):
        after = [(arrived,) if slot == 2 else (), ()]
        sent = [[step(slot, flow, k, (0, 4), after[k]) for k in range(2)] for flow in range(2)]
        for flow in range(2):
            got[flow].append([send(x, flow) for x in sent[flow]])

    def weights_of(slots):
        weights = []
        for k in range(2):
            for slot in slots:
                if slot:
                    weights += [got[0][slot - 1][k], got[1][line - slot - 1][k]]
                else:
                    weights.append(first[k])
        return weights

    early_slots = [slot for slot in range(line) if slot not in (1, line - 1)]
    late_slots = [slot for slot in range(line) if slot not in early_slots]
    early = [
        product_call(
            place, both_grads, weights_of(early_slots), early_slots, (), (), F32, flip, line, "early", ()
        )
        for flip in (1, 0)
    ]

    own = own_call(place, hidden, out_grads, block, line)
    sent = [
        [
            step(line, flow, 0, (0, 4), (own,)),
            step(line, flow, 1, (0, 3), (early[0][1], early[1][1])),
        ]
        for flow in range(2)
    ]
    last = [[send(x, flow) for x in sent[flow]] for flow in range(2)]
    sent = sent[0] + sent[1]

    late = weights_of(late_slots)
    product, token = product_call(
        place, both_grads, late, late_slots, (early[0][0],), (), BF16, 1, line, "product", sent
    )
    from_sib = swap(product)
    *grads, token = product_call(
        place, both_grads, late, late_slots, (early[1][0],), (gate_pre, up_pre), None, 0, line, "grads", [token]
    )

    for flow in range(2):
        last[flow].append(send(step(line, flow, 1, (3, 4), (token,)), flow))
    one, two = last
    grad_down, token = final_call(place, one[0], two[0], own, 0, line, scale, (), (token,))
    grads = join_call(place, from_sib, gate_pre, up_pre, *grads, [token])
    grad_down, _ = final_call(
        place, one[1], two[1], own, 4, line, scale, (grad_down,), tuple(grads)
    )
    at = along(place, 0, line)
    start = units - units // 8
    total = own[start:].astype(F32)
    total += jnp.where(at > 0, one[2].astype(F32), 0.0)
    total += jnp.where(at < line - 1, two[2].astype(F32), 0.0)
    piece = (total * scale).astype(BF16)
    grad_down = lax.dynamic_update_slice_in_dim(grad_down, piece, start, axis=0)
    return (*grads, grad_down)


def solution(mesh):
    return jax.shard_map(
        shards,
        mesh=mesh,
        in_specs=(P(("dp", "mp"), None), P("dp", "mp"), P("dp", "mp"), P("mp", "dp")),
        out_specs=(P("dp", "mp"), P("dp", "mp"), P("mp", "dp")),
        check_vma=False,
    )
```
